32 devices in a mesh: kern: 4 (over x, core), slab: 8 (over z, y).
Axes of the slice: x: 2, y: 2, z: 4, core: 2. Of those that a mesh axis runs over, the one named last changes fastest.
Arguments:
- layout: int32 [4096, 4096], P('slab', 'kern'), may hold values 0 or 1
- band_freqs: int32 [128], replicated, may hold values from -256 to 255, as said below
- kernels: float32 [2, 48, 128, 128], P(None, 'kern'), may hold values from -6 to 6
- eigen_values: float32 [48], P('kern'), may hold values from 0.1 to 1
- bake_rates: float32 [5], replicated, may hold values from 0.1 to 0.25
Outputs:
- aerial_image: float32 [4096, 4096], P('slab', 'kern')
- latent_acid: float32 [4096, 4096], P('slab', 'kern')
The draws below stay inside these ranges and needn't reach their ends.
Inputs may be any that keep to these rules, and one draw needn't show every extreme that they name: `band_freqs`: the 128 numbers are distinct; both ends of the range are among them.
All inputs are finite; a program needn't handle non-finite values. No bound on the sum of `layout` on one device may be relied on, other than what follows from the above.
Results may differ from the reference program's by a relative error of at most 0.0017.
Values sent between devices are 32-bit elements; how exact they have to be, the bound alone decides.
A program may use at most 128 MiB of HBM per device.

```python
import math
import jax
import jax.numpy as jnp
from jax import lax

N = 4096
W = 128
FIELDS = 48
STEPS = 2


def draw_band_freqs(key, part):
    shuffled = jax.random.permutation(key, 4 * W - 2)[:W - 2].astype(jnp.int32) - 2 * W + 1
    ends = jnp.array([-2 * W, 2 * W - 1], dtype=jnp.int32)
    return jnp.concatenate([ends, shuffled]).astype(jnp.int32)


def set_ends(entries, own_key, smallest, largest):
    dims = entries.shape
    spot = [jax.random.randint(jax.random.fold_in(own_key, axis), (), 0, dims[axis]) for axis in range(len(dims))]
    entries = entries.at[tuple(spot)].set(smallest)
    longest = dims.index(max(dims))
    spot[longest] = (spot[longest] + 1) % dims[longest]
    return entries.at[tuple(spot)].set(largest)


def block_scale(key, dims, shards, least, largest):
    level = 1.0
    for dim, blocks in shards:
        steps = jax.random.uniform(jax.random.fold_in(jax.random.fold_in(key, 6), dim), (blocks,), jnp.float32, least / len(shards), largest / len(shards))
        level = level * jnp.repeat(jnp.exp(steps), dims[dim] // blocks).reshape((-1,) + (1,) * (len(dims) - 1 - dim))
    return level


def normal_values(own_key, dims, spread, bound, cuts=(), kind=jnp.bfloat16):
    values = jax.random.normal(own_key, dims, jnp.float32) * spread
    if len(cuts) > 0:
        values = block_scale(own_key, dims, cuts, -0.22, 0.18) * values
    return jnp.clip(values, min=-bound, max=bound).astype(kind)


def setup_inputs(seed: int = 0) -> dict:
    keys = jax.random.split(jax.random.key(seed), 6)
    return {
        "layout": set_ends((jax.random.randint(keys[0], (N, N), 0, 2) < 1).astype(jnp.int32), jax.random.fold_in(keys[0], 1), 0, 1),
        "band_freqs": draw_band_freqs(jax.random.fold_in(keys[5], 71), 0),
        "kernels": normal_values(keys[2], (2, FIELDS, W, W), 1.0, 6.0, ((1, 4),), jnp.float32),
        "eigen_values": jnp.clip(jnp.exp(math.log(1.0) - 2.3025851 * jax.random.uniform(keys[3], (FIELDS,), jnp.float32) ** block_scale(keys[3], (FIELDS,), ((0, 4),), -0.2, 0.2)), 0.1, 1.0),
        "bake_rates": jnp.clip(jnp.exp(jax.random.uniform(keys[4], (5,), jnp.float32, math.log(0.1), math.log(0.25))), 0.1, 0.25),
    }


highest = lax.Precision.HIGHEST


def tables(frequencies, first_index, length):
    positions = first_index + jnp.arange(length, dtype=jnp.int32)
    angles = jnp.mod(positions[:, None] * frequencies[None, :], N).astype(jnp.float32) * (2.0 * math.pi / N)
    return jnp.cos(angles), jnp.sin(angles)


def laplace(field):
    return (jnp.roll(field, 1, 0) + jnp.roll(field, -1, 0) + jnp.roll(field, 1, 1)
            + jnp.roll(field, -1, 1) - 4.0 * field)


def reference(layout, band_freqs, kernels, eigen_values, bake_rates):
    transmit = (2 * layout - 1).astype(jnp.float32)
    cos_all, sin_all = tables(band_freqs, 0, N)
    along_re = jnp.dot(transmit, cos_all, precision=highest)
    along_im = -jnp.dot(transmit, sin_all, precision=highest)
    spec_re = (jnp.dot(cos_all.T, along_re, precision=highest) + jnp.dot(sin_all.T, along_im, precision=highest)) / N
    spec_im = (jnp.dot(cos_all.T, along_im, precision=highest) - jnp.dot(sin_all.T, along_re, precision=highest)) / N
    row_table = jnp.concatenate([cos_all, sin_all], 1).astype(jnp.bfloat16).astype(jnp.float32)
    col_table = jnp.concatenate([jnp.concatenate([cos_all.T, sin_all.T], 1),
                                 jnp.concatenate([-sin_all.T, cos_all.T], 1)], 0)
    col_table = col_table.astype(jnp.bfloat16).astype(jnp.float32)

    def one_field(total_sum, field_item):
        kern_re, kern_im, eigen_one = field_item
        prod_re = spec_re * kern_re - spec_im * kern_im
        prod_im = spec_re * kern_im + spec_im * kern_re
        spectral_block = jnp.concatenate([jnp.concatenate([prod_re, prod_im], 1),
                                          jnp.concatenate([-prod_im, prod_re], 1)], 0)
        spectral_block = spectral_block.astype(jnp.bfloat16).astype(jnp.float32)
        row_field = (jnp.dot(row_table, spectral_block, preferred_element_type=jnp.float32) / W)
        row_field = row_field.astype(jnp.bfloat16).astype(jnp.float32)
        field_pair = jnp.dot(row_field, col_table, preferred_element_type=jnp.float32)
        power = field_pair[:, :N] * field_pair[:, :N] + field_pair[:, N:] * field_pair[:, N:]
        return total_sum + eigen_one * power, None

    total_sum, unused = lax.scan(one_field, jnp.zeros((N, N), jnp.float32),
                                 (kernels[0], kernels[1], eigen_values))
    aerial_image = total_sum / FIELDS
    dill_rate, acid_rate, quench_rate, react_rate, quench_start = (bake_rates[0], bake_rates[1], bake_rates[2], bake_rates[3], bake_rates[4])
    acid_field = 1.0 - jnp.exp(-4.0 * dill_rate * aerial_image)
    acid_diffusion = acid_rate * (0.5 + 0.5 * acid_field)
    quencher = jnp.zeros_like(acid_field) + quench_start
    for bake_step in range(STEPS):
        reaction = 4.0 * react_rate * acid_field * quencher
        new_acid = acid_field + acid_diffusion * laplace(acid_field) - reaction
        quencher = quencher + quench_rate * laplace(quencher) - reaction
        acid_field = new_acid
    return aerial_image, acid_field
```

```python
import functools
import math

import jax
import jax.numpy as jnp
import numpy as np
from jax import lax
from jax.experimental import pallas as pl
from jax.experimental.pallas import tpu as pltpu
from jax.sharding import PartitionSpec as P

BAND = 256
COARSE = 4 * BAND
HALO = 8
SIDE = 64
f32 = jnp.float32
bf16 = jnp.bfloat16


def trig(count, total):
    m = count & (total - 1)
    quarter = total // 4
    quad = (m + quarter // 2) >> (quarter.bit_length() - 1)
    rest = m - quad * quarter
    x = rest.astype(f32) * (2.0 * math.pi / total)
    y = x * x
    s = x * (1.0 + y * (-1.0 / 6 + y * (1.0 / 120 + y * (-1.0 / 5040 + y * (1.0 / 362880)))))
    c = 1.0 + y * (-0.5 + y * (1.0 / 24 + y * (-1.0 / 720 + y * (1.0 / 40320 + y * (-1.0 / 3628800)))))
    odd = (quad & 1) == 1
    cos = jnp.where(odd, s, c)
    sin = jnp.where(odd, c, s)
    cos = jnp.where(((quad + 1) & 2) == 2, -cos, cos)
    sin = jnp.where((quad & 2) == 2, -sin, sin)
    return cos, sin


def split(a):
    hi = a.astype(bf16)
    return hi, (a - hi.astype(f32)).astype(bf16)


def dot(a, b):
    return jnp.dot(a, b, preferred_element_type=f32)


def row_chunk(ext):
    return max(c for c in range(16, 97, 16) if ext % c == 0)


def image_kernel(
    n_kern, n_slab, layout_ref, frow_ref, fcol_ref, kern_ref, eig_ref, out_ref,
    kb, colw, rowt_h, rowt_l, rowb, ct, part, recv_a, recv_b, spec, rf, acc, recv_s,
    send_k, recv_k, send_a, rsem_a, send_b, rsem_b, send_c, rsem_c, send_s, rsem_s,
):
    rows, cols = layout_ref.shape
    n = cols * n_kern
    fields = kern_ref.shape[1]
    w = kern_ref.shape[2]
    half = n_kern // 2
    ext = rows + 2 * HALO
    piece = 2 * w // n_slab
    my_k = lax.axis_index("kern")
    my_s = lax.axis_index("slab")
    my_h = my_k // 2
    core = my_k % 2

    def slab_peer(d):
        return lax.rem(my_s + d, n_slab)

    def kern_peer(d):
        return lax.rem(my_k + d, n_kern)

    barrier = pltpu.get_barrier_semaphore()

    @pl.loop(1, n_slab)
    def _(d):
        pl.semaphore_signal(barrier, inc=1, device_id={"slab": slab_peer(d)}, device_id_type=pl.DeviceIdType.MESH)

    for d in range(1, n_kern):
        pl.semaphore_signal(barrier, inc=1, device_id={"kern": kern_peer(d)}, device_id_type=pl.DeviceIdType.MESH)

    for f in range(fields):
        for c in range(2):
            kb[my_h, f, c] = kern_ref[c, f] * eig_ref[f]
    pl.semaphore_wait(barrier, n_slab - 1 + n_kern - 1)

    def kern_copy(d):
        return pltpu.make_async_remote_copy(
            src_ref=kb.at[my_h], dst_ref=kb.at[my_h],
            send_sem=send_k.at[d - 1], recv_sem=recv_k.at[d - 1],
            device_id={"kern": lax.rem(my_h + d, half) * 2 + core}, device_id_type=pl.DeviceIdType.MESH)

    for d in range(1, half):
        kern_copy(d).start()

    pos = my_k * cols + lax.broadcasted_iota(jnp.int32, (cols, w), 0)
    cos, sin = trig(pos * frow_ref[...], n)
    ch, cl = split(cos)
    sh, sl = split(sin)
    colw[:, 0:w] = ch
    colw[:, w:2 * w] = sh
    colw[:, 2 * w:3 * w] = cl
    colw[:, 3 * w:4 * w] = sl
    pos = my_s * rows + lax.broadcasted_iota(jnp.int32, (w, rows), 1)
    cos, sin = trig(pos * fcol_ref[...], n)
    ch, cl = split(cos)
    sh, sl = split(sin)
    rowt_h[0:w] = ch
    rowt_h[w:2 * w] = sh
    rowt_l[0:w] = cl
    rowt_l[w:2 * w] = sl
    x = (2 * layout_ref[...] - 1).astype(f32).astype(bf16)
    along = dot(x, colw[...])
    ah, al = split(along[:, :2 * w] + along[:, 2 * w:])
    both = dot(rowt_h[...], ah) + (dot(rowt_h[...], al) + dot(rowt_l[...], ah))
    re = (both[:w, :w] - both[w:, w:]) * (1.0 / n)
    im = (both[:w, w:] + both[w:, :w]) * (-1.0 / n)
    full = jnp.concatenate([re, im], 0)
    for i in range(n_slab):
        part[i] = full[i * piece:(i + 1) * piece]

    def copy_a(d):
        return pltpu.make_async_remote_copy(
            src_ref=part.at[slab_peer(d)], dst_ref=recv_a.at[d - 1],
            send_sem=send_a.at[d - 1], recv_sem=rsem_a.at[d - 1],
            device_id={"slab": slab_peer(d)}, device_id_type=pl.DeviceIdType.MESH)

    @pl.loop(1, n_slab)
    def _(d):
        copy_a(d).start()

    r = lax.broadcasted_iota(jnp.int32, (ext, w), 0)
    pos = my_s * rows + jnp.where(r < rows + HALO, r, r - ext)
    cos, sin = trig(pos * frow_ref[...], n)
    rowb[:, 0:w] = cos.astype(bf16)
    rowb[:, w:2 * w] = sin.astype(bf16)
    block = COARSE // n_kern
    for j in range(n_kern):
        pos = (n // COARSE) * (j * block + lax.broadcasted_iota(jnp.int32, (w, block), 1))
        cos, sin = trig(pos * fcol_ref[...], n)
        ct[j, 0:w, 0:block] = cos.astype(bf16)
        ct[j, 0:w, block:2 * block] = sin.astype(bf16)
        ct[j, w:2 * w, 0:block] = (-sin).astype(bf16)
        ct[j, w:2 * w, block:2 * block] = cos.astype(bf16)

    @pl.loop(1, n_slab)
    def _(d):
        copy_a(d).wait()

    total = part[my_s]
    for d in range(1, n_slab):
        total = total + recv_a[d - 1]
    recv_b[my_k] = total

    def copy_b(d):
        return pltpu.make_async_remote_copy(
            src_ref=recv_b.at[my_k], dst_ref=recv_b.at[my_k],
            send_sem=send_b.at[d - 1], recv_sem=rsem_b.at[d - 1],
            device_id={"kern": kern_peer(d)}, device_id_type=pl.DeviceIdType.MESH)

    for d in range(1, n_kern):
        copy_b(d).start()
    for d in range(1, n_kern):
        copy_b(d).wait()
    total = recv_b[0]
    for k in range(1, n_kern):
        total = total + recv_b[k]
    spec[my_s] = total

    def copy_c(d):
        return pltpu.make_async_remote_copy(
            src_ref=spec.at[my_s], dst_ref=spec.at[my_s],
            send_sem=send_c.at[d - 1], recv_sem=rsem_c.at[d - 1],
            device_id={"slab": slab_peer(d)}, device_id_type=pl.DeviceIdType.MESH)

    @pl.loop(1, n_slab)
    def _(d):
        copy_c(d).start()

    @pl.loop(1, n_slab)
    def _(d):
        copy_c(d).wait()

    for d in range(1, half):
        kern_copy(d).wait()

    full = jnp.concatenate([spec[i] for i in range(n_slab)], 0)
    spec_re = full[:w]
    spec_im = full[w:]
    step = row_chunk(ext)
    chunks = ext // step
    count = half * fields

    for h in range(half):
        @pl.loop(0, fields)
        def _(f):
            kr = kb[h, f, 0]
            ki = kb[h, f, 1]
            pr = (spec_re * kr - spec_im * ki)
            pi = (spec_re * ki + spec_im * kr)
            prod = jnp.concatenate(
                [jnp.concatenate([pr, pi], 1), jnp.concatenate([-pi, pr], 1)], 0).astype(bf16)
            field = (dot(rowb[...], prod) * (1.0 / w)).astype(bf16)
            at = pl.multiple_of((h * fields + f) * step, 16)
            for i in range(chunks):
                rf[i, pl.ds(at, step), :] = field[i * step:(i + 1) * step]

    partner = my_k + 1 - 2 * core

    def copy_s(j):
        return pltpu.make_async_remote_copy(
            src_ref=acc.at[j], dst_ref=recv_s.at[j],
            send_sem=send_s.at[j], recv_sem=rsem_s.at[j],
            device_id={"kern": partner}, device_id_type=pl.DeviceIdType.MESH)

    @pl.loop(0, n_kern)
    def _(j):
        @pl.loop(0, chunks)
        def _(i):
            e = dot(rf[i], ct[j])
            total = None
            for f in range(count):
                one = e[f * step:(f + 1) * step]
                sq = one * one
                sq = sq[:, :block] + sq[:, block:]
                total = sq if total is None else total + sq
            acc[j, pl.ds(pl.multiple_of(i * step, 16), step), :] = total

        copy_s(j).start()

    for j in range(n_kern):
        copy_s(j).wait()
        out_ref[lax.rem(j + n_kern - my_k, n_kern)] = acc[j] + recv_s[j]


def bake_kernel(fields, coarse_ref, dh_ref, dl_ref, rates_ref, aer_ref, lat_ref, xh, xl, aer, acid0, acid1):
    n_kern, ext, block = coarse_ref.shape
    rows, cols = aer_ref.shape
    wide = dh_ref.shape[1]
    step = row_chunk(ext)
    chunks = ext // step
    dill, arate, react, qstart = rates_ref[0], rates_ref[1], rates_ref[3], rates_ref[4]
    for j in range(n_kern):
        hi, lo = split(coarse_ref[j])
        xh[:, j * block:(j + 1) * block] = hi
        xl[:, j * block:(j + 1) * block] = lo
    tile = 384 if wide % 384 == 0 else 128
    for c in range(0, wide, tile):
        s = slice(c, c + tile)
        aer[:, s] = (dot(xh[...], dh_ref[:, s]) + (dot(xl[...], dh_ref[:, s]) + dot(xh[...], dl_ref[:, s]))) * (
            1.0 / fields)

    @pl.loop(0, chunks)
    def _(i):
        at = pl.ds(pl.multiple_of(i * step, 16), step)
        acid0[at, :] = 1.0 - jnp.exp((-4.0 * dill) * aer[at, :])

    aer_ref[...] = aer[0:rows, 0:cols]

    def laplace(ref, i):
        first = i * step
        mid = ref[pl.ds(pl.multiple_of(first, 8), step), :]
        before = ref[pl.ds(pl.multiple_of(lax.rem(first + ext - 8, ext), 8), 8), :]
        after = ref[pl.ds(pl.multiple_of(lax.rem(first + step, ext), 8), 8), :]
        tall = jnp.concatenate([before, mid, after], 0)
        up = pltpu.roll(tall, 1, 0)[8:8 + step]
        down = pltpu.roll(tall, step + 15, 0)[8:8 + step]
        left = pltpu.roll(mid, 1, 1)
        right = pltpu.roll(mid, wide - 1, 1)
        return mid, down + up + right + left - 4.0 * mid

    @pl.loop(0, chunks)
    def _(i):
        mid, lap = laplace(acid0, i)
        value = mid + (arate * (0.5 + 0.5 * mid)) * lap - 4.0 * react * mid * qstart
        acid1[pl.ds(pl.multiple_of(i * step, 16), step), :] = value

    @pl.loop(0, chunks)
    def _(i):
        at = pl.ds(pl.multiple_of(i * step, 16), step)
        mid, lap = laplace(acid1, i)
        first = acid0[at, :]
        quench = qstart - 4.0 * react * first * qstart
        aer[at, :] = mid + (arate * (0.5 + 0.5 * first)) * lap - 4.0 * react * mid * quench

    lat_ref[...] = aer[0:rows, 0:cols]


def interpolation(cols, n):
    wide = cols + 2 * SIDE
    c = np.arange(wide)
    c = np.where(c < cols + SIDE, c, c - wide)
    ratio = n // COARSE
    t = c[None, :] - ratio * np.arange(COARSE)[:, None]
    zero = t % n == 0
    safe = np.where(zero, 1, t)
    d = np.sin(np.pi * (safe % (2 * ratio)) / ratio) / (COARSE * np.tan(np.pi * safe / n))
    d = np.where(zero, 1.0, np.where(t % ratio == 0, 0.0, d))
    hi = d.astype(jnp.bfloat16)
    lo = (d - hi.astype(np.float64)).astype(jnp.bfloat16)
    return hi, lo


def shards(n_kern, n_slab, layout, band_freqs, kernels, eigen_values, bake_rates):
    rows, cols = layout.shape
    fields, w = kernels.shape[1], kernels.shape[2]
    n = cols * n_kern
    ext = rows + 2 * HALO
    half = n_kern // 2
    block = COARSE // n_kern
    piece = 2 * w // n_slab
    step = row_chunk(ext)
    chunks = ext // step
    eig = jnp.broadcast_to(jnp.sqrt(eigen_values)[:, None, None], (fields, 1, w))
    vmem = pl.BlockSpec(memory_space=pltpu.VMEM)
    dma = pltpu.SemaphoreType.DMA
    coarse = pl.pallas_call(
        functools.partial(image_kernel, n_kern, n_slab),
        out_shape=jax.ShapeDtypeStruct((n_kern, ext, block), f32),
        in_specs=[vmem] * 5,
        out_specs=vmem,
        scratch_shapes=[
            pltpu.VMEM((half, fields, 2, w, w), f32),
            pltpu.VMEM((cols, 4 * w), bf16),
            pltpu.VMEM((2 * w, rows), bf16),
            pltpu.VMEM((2 * w, rows), bf16),
            pltpu.VMEM((ext, 2 * w), bf16),
            pltpu.VMEM((n_kern, 2 * w, 2 * block), bf16),
            pltpu.VMEM((n_slab, piece, w), f32),
            pltpu.VMEM((n_slab - 1, piece, w), f32),
            pltpu.VMEM((n_kern, piece, w), f32),
            pltpu.VMEM((n_slab, piece, w), f32),
            pltpu.VMEM((chunks, half * fields * step, 2 * w), bf16),
            pltpu.VMEM((n_kern, ext, block), f32),
            pltpu.VMEM((n_kern, ext, block), f32),
            dma((half,)), dma((half,)),
            dma((n_slab - 1,)), dma((n_slab - 1,)),
            dma((n_kern - 1,)), dma((n_kern - 1,)),
            dma((n_slab - 1,)), dma((n_slab - 1,)),
            dma((n_kern,)), dma((n_kern,)),
        ],
        compiler_params=pltpu.CompilerParams(
            collective_id=0, has_side_effects=True, vmem_limit_bytes=56 * 2**20),
        name="coarse_image",
    )(layout, band_freqs.reshape(1, w), band_freqs.reshape(w, 1), kernels, eig)
    dh, dl = interpolation(cols, n)
    wide = cols + 2 * SIDE
    return pl.pallas_call(
        functools.partial(bake_kernel, fields * n_kern),
        out_shape=[jax.ShapeDtypeStruct((rows, cols), f32)] * 2,
        in_specs=[vmem, vmem, vmem, pl.BlockSpec(memory_space=pltpu.SMEM)],
        out_specs=[vmem, vmem],
        scratch_shapes=[
            pltpu.VMEM((ext, COARSE), bf16),
            pltpu.VMEM((ext, COARSE), bf16),
            pltpu.VMEM((ext, wide), f32),
            pltpu.VMEM((ext, wide), f32),
            pltpu.VMEM((ext, wide), f32),
        ],
        compiler_params=pltpu.CompilerParams(vmem_limit_bytes=56 * 2**20),
        name="interpolate_bake",
    )(coarse, jnp.asarray(dh), jnp.asarray(dl), bake_rates)


def solution(mesh):
    return jax.shard_map(
        functools.partial(shards, mesh.shape["kern"], mesh.shape["slab"]),
        mesh=mesh,
        in_specs=(P("slab", "kern"), P(), P(None, "kern", None, None), P("kern"), P()),
        out_specs=(P("slab", "kern"), P("slab", "kern")),
        check_vma=False,
    )
```

```python
import functools
import math

import jax
import jax.numpy as jnp
import numpy as np
from jax import lax
from jax.experimental import pallas as pl
from jax.experimental.pallas import tpu as pltpu
from jax.sharding import PartitionSpec as P

BAND = 256
COARSE = 4 * BAND
HALO = 8
SIDE = 64
f32 = jnp.float32
bf16 = jnp.bfloat16


def trig(count, total):
    m = count & (total - 1)
    quarter = total // 4
    quad = (m + quarter // 2) >> (quarter.bit_length() - 1)
    rest = m - quad * quarter
    x = rest.astype(f32) * (2.0 * math.pi / total)
    y = x * x
    s = x * (1.0 + y * (-1.0 / 6 + y * (1.0 / 120 + y * (-1.0 / 5040 + y * (1.0 / 362880)))))
    c = 1.0 + y * (-0.5 + y * (1.0 / 24 + y * (-1.0 / 720 + y * (1.0 / 40320 + y * (-1.0 / 3628800)))))
    odd = (quad & 1) == 1
    cos = jnp.where(odd, s, c)
    sin = jnp.where(odd, c, s)
    cos = jnp.where(((quad + 1) & 2) == 2, -cos, cos)
    sin = jnp.where((quad & 2) == 2, -sin, sin)
    return cos, sin


def split(a):
    hi = a.astype(bf16)
    return hi, (a - hi.astype(f32)).astype(bf16)


def dot(a, b):
    return jnp.dot(a, b, preferred_element_type=f32)


def row_chunk(ext):
    return max(c for c in range(16, 97, 16) if ext % c == 0)


def image_kernel(
    n_kern, n_slab, layout_ref, frow_ref, kern_ref, eig_ref, out_ref,
    kb, colw, rowt_h, rowt_l, rowb, ct, part, recv_a, recv_b, spec, rf, acc, recv_s,
    send_k, recv_k, send_a, rsem_a, send_b, rsem_b, send_c, rsem_c, send_s, rsem_s,
):
    rows, cols = layout_ref.shape
    n = cols * n_kern
    fields = kern_ref.shape[1]
    w = kern_ref.shape[2]
    half = n_kern // 2
    ext = rows + 2 * HALO
    piece = 2 * w // n_slab
    my_k = lax.axis_index("kern")
    my_s = lax.axis_index("slab")
    my_h = my_k // 2
    core = my_k % 2

    def slab_peer(d):
        return lax.rem(my_s + d, n_slab)

    def kern_peer(d):
        return lax.rem(my_k + d, n_kern)

    barrier = pltpu.get_barrier_semaphore()

    @pl.loop(1, n_slab)
    def _(d):
        pl.semaphore_signal(barrier, inc=1, device_id={"slab": slab_peer(d)}, device_id_type=pl.DeviceIdType.MESH)

    for d in range(1, n_kern):
        pl.semaphore_signal(barrier, inc=1, device_id={"kern": kern_peer(d)}, device_id_type=pl.DeviceIdType.MESH)

    for f in range(fields):
        weight = jnp.sqrt(jnp.full((1, w), eig_ref[f], f32))
        for c in range(2):
            kb[my_h, f, c] = kern_ref[c, f] * weight
    pl.semaphore_wait(barrier, n_slab - 1 + n_kern - 1)

    def kern_copy(d):
        return pltpu.make_async_remote_copy(
            src_ref=kb.at[my_h], dst_ref=kb.at[my_h],
            send_sem=send_k.at[d - 1], recv_sem=recv_k.at[d - 1],
            device_id={"kern": lax.rem(my_h + d, half) * 2 + core}, device_id_type=pl.DeviceIdType.MESH)

    for d in range(1, half):
        kern_copy(d).start()

    fcol = jnp.transpose(jnp.broadcast_to(frow_ref[...], (w, w)))[:, 0:1]
    pos = my_k * cols + lax.broadcasted_iota(jnp.int32, (cols, w), 0)
    cos, sin = trig(pos * frow_ref[...], n)
    ch, cl = split(cos)
    sh, sl = split(sin)
    colw[:, 0:w] = ch
    colw[:, w:2 * w] = sh
    colw[:, 2 * w:3 * w] = cl
    colw[:, 3 * w:4 * w] = sl
    pos = my_s * rows + lax.broadcasted_iota(jnp.int32, (w, rows), 1)
    cos, sin = trig(pos * fcol, n)
    ch, cl = split(cos)
    sh, sl = split(sin)
    rowt_h[0:w] = ch
    rowt_h[w:2 * w] = sh
    rowt_l[0:w] = cl
    rowt_l[w:2 * w] = sl
    x = (2 * layout_ref[...] - 1).astype(f32).astype(bf16)
    along = dot(x, colw[...])
    ah, al = split(along[:, :2 * w] + along[:, 2 * w:])
    both = dot(rowt_h[...], ah) + (dot(rowt_h[...], al) + dot(rowt_l[...], ah))
    re = (both[:w, :w] - both[w:, w:]) * (1.0 / n)
    im = (both[:w, w:] + both[w:, :w]) * (-1.0 / n)
    full = jnp.concatenate([re, im], 0)
    for i in range(n_slab):
        part[i] = full[i * piece:(i + 1) * piece]

    def copy_a(d):
        return pltpu.make_async_remote_copy(
            src_ref=part.at[slab_peer(d)], dst_ref=recv_a.at[d - 1],
            send_sem=send_a.at[d - 1], recv_sem=rsem_a.at[d - 1],
            device_id={"slab": slab_peer(d)}, device_id_type=pl.DeviceIdType.MESH)

    @pl.loop(1, n_slab)
    def _(d):
        copy_a(d).start()

    r = lax.broadcasted_iota(jnp.int32, (ext, w), 0)
    pos = my_s * rows + jnp.where(r < rows + HALO, r, r - ext)
    cos, sin = trig(pos * frow_ref[...], n)
    rowb[:, 0:w] = cos.astype(bf16)
    rowb[:, w:2 * w] = sin.astype(bf16)
    block = COARSE // n_kern
    for j in range(n_kern):
        pos = (n // COARSE) * (j * block + lax.broadcasted_iota(jnp.int32, (w, block), 1))
        cos, sin = trig(pos * fcol, n)
        ct[j, 0:w, 0:block] = cos.astype(bf16)
        ct[j, 0:w, block:2 * block] = sin.astype(bf16)
        ct[j, w:2 * w, 0:block] = (-sin).astype(bf16)
        ct[j, w:2 * w, block:2 * block] = cos.astype(bf16)

    @pl.loop(1, n_slab)
    def _(d):
        copy_a(d).wait()

    total = part[my_s]
    for d in range(1, n_slab):
        total = total + recv_a[d - 1]
    recv_b[my_k] = total

    def copy_b(d):
        return pltpu.make_async_remote_copy(
            src_ref=recv_b.at[my_k], dst_ref=recv_b.at[my_k],
            send_sem=send_b.at[d - 1], recv_sem=rsem_b.at[d - 1],
            device_id={"kern": kern_peer(d)}, device_id_type=pl.DeviceIdType.MESH)

    for d in range(1, n_kern):
        copy_b(d).start()
    for d in range(1, n_kern):
        copy_b(d).wait()
    total = recv_b[0]
    for k in range(1, n_kern):
        total = total + recv_b[k]
    spec[my_s] = total

    def copy_c(d):
        return pltpu.make_async_remote_copy(
            src_ref=spec.at[my_s], dst_ref=spec.at[my_s],
            send_sem=send_c.at[d - 1], recv_sem=rsem_c.at[d - 1],
            device_id={"slab": slab_peer(d)}, device_id_type=pl.DeviceIdType.MESH)

    @pl.loop(1, n_slab)
    def _(d):
        copy_c(d).start()

    @pl.loop(1, n_slab)
    def _(d):
        copy_c(d).wait()

    full = jnp.concatenate([spec[i] for i in range(n_slab)], 0)
    spec_re = full[:w]
    spec_im = full[w:]
    step = row_chunk(ext)
    chunks = ext // step
    partner = my_k + 1 - 2 * core

    def copy_s(j):
        return pltpu.make_async_remote_copy(
            src_ref=acc.at[j], dst_ref=recv_s.at[j],
            send_sem=send_s.at[j], recv_sem=rsem_s.at[j],
            device_id={"kern": partner}, device_id_type=pl.DeviceIdType.MESH)

    for phase in range(half):
        h = lax.rem(my_h + half - phase, half)
        if phase > 0:
            kern_copy(phase).wait()

        @pl.loop(0, fields)
        def _(f):
            kr = kb[h, f, 0]
            ki = kb[h, f, 1]
            pr = spec_re * kr - spec_im * ki
            pi = spec_re * ki + spec_im * kr
            prod = jnp.concatenate(
                [jnp.concatenate([pr, pi], 1), jnp.concatenate([-pi, pr], 1)], 0).astype(bf16)
            field = (dot(rowb[...], prod) * (1.0 / w)).astype(bf16)
            at = pl.multiple_of(f * step, 16)
            for i in range(chunks):
                rf[i, pl.ds(at, step), :] = field[i * step:(i + 1) * step]

        @pl.loop(0, n_kern)
        def _(j):
            @pl.loop(0, chunks)
            def _(i):
                at = pl.ds(pl.multiple_of(i * step, 16), step)
                e = dot(rf[i], ct[j])
                total = None if phase == 0 else acc[j, at, :]
                for f in range(fields):
                    one = e[f * step:(f + 1) * step]
                    sq = one * one
                    sq = sq[:, :block] + sq[:, block:]
                    total = sq if total is None else total + sq
                acc[j, at, :] = total

            if phase == half - 1:
                copy_s(j).start()

    for j in range(n_kern):
        copy_s(j).wait()
        out_ref[lax.rem(j + n_kern - my_k, n_kern)] = acc[j] + recv_s[j]


def bake_kernel(fields, coarse_ref, dh_ref, dl_ref, rates_ref, aer_ref, lat_ref, xs, aer, acid0, acid1):
    n_kern, ext, block = coarse_ref.shape
    rows, cols = aer_ref.shape
    wide = dh_ref.shape[1]
    step = row_chunk(ext)
    chunks = ext // step
    dill, arate, react, qstart = rates_ref[0], rates_ref[1], rates_ref[3], rates_ref[4]
    for j in range(n_kern):
        hi, lo = split(coarse_ref[j])
        xs[0:ext, j * block:(j + 1) * block] = hi
        xs[ext:2 * ext, j * block:(j + 1) * block] = lo
    tile = 384 if wide % 384 == 0 else 128
    for c in range(0, wide, tile):
        s = slice(c, c + tile)
        both = dot(xs[...], dh_ref[:, s])
        value = (both[:ext] + (both[ext:] + dot(xs[0:ext, :], dl_ref[:, s]))) * (1.0 / fields)
        aer[:, s] = value
        acid0[:, s] = 1.0 - jnp.exp((-4.0 * dill) * value)

    aer_ref[...] = aer[0:rows, 0:cols]

    def laplace(ref, i):
        first = i * step
        mid = ref[pl.ds(pl.multiple_of(first, 8), step), :]
        before = ref[pl.ds(pl.multiple_of(lax.rem(first + ext - 8, ext), 8), 8), :]
        after = ref[pl.ds(pl.multiple_of(lax.rem(first + step, ext), 8), 8), :]
        tall = jnp.concatenate([before, mid, after], 0)
        up = pltpu.roll(tall, 1, 0)[8:8 + step]
        down = pltpu.roll(tall, step + 15, 0)[8:8 + step]
        left = pltpu.roll(mid, 1, 1)
        right = pltpu.roll(mid, wide - 1, 1)
        return mid, down + up + right + left - 4.0 * mid

    @pl.loop(0, chunks)
    def _(i):
        mid, lap = laplace(acid0, i)
        value = mid + (arate * (0.5 + 0.5 * mid)) * lap - 4.0 * react * mid * qstart
        acid1[pl.ds(pl.multiple_of(i * step, 16), step), :] = value

    @pl.loop(0, chunks)
    def _(i):
        at = pl.ds(pl.multiple_of(i * step, 16), step)
        mid, lap = laplace(acid1, i)
        first = acid0[at, :]
        quench = qstart - 4.0 * react * first * qstart
        aer[at, :] = mid + (arate * (0.5 + 0.5 * first)) * lap - 4.0 * react * mid * quench

    lat_ref[...] = aer[0:rows, 0:cols]


def interpolation(cols, n):
    wide = cols + 2 * SIDE
    c = np.arange(wide)
    c = np.where(c < cols + SIDE, c, c - wide)
    ratio = n // COARSE
    t = c[None, :] - ratio * np.arange(COARSE)[:, None]
    zero = t % n == 0
    safe = np.where(zero, 1, t)
    d = np.sin(np.pi * (safe % (2 * ratio)) / ratio) / (COARSE * np.tan(np.pi * safe / n))
    d = np.where(zero, 1.0, np.where(t % ratio == 0, 0.0, d))
    hi = d.astype(jnp.bfloat16)
    lo = (d - hi.astype(np.float64)).astype(jnp.bfloat16)
    return hi, lo


def shards(n_kern, n_slab, layout, band_freqs, kernels, eigen_values, bake_rates):
    rows, cols = layout.shape
    fields, w = kernels.shape[1], kernels.shape[2]
    n = cols * n_kern
    ext = rows + 2 * HALO
    half = n_kern // 2
    block = COARSE // n_kern
    piece = 2 * w // n_slab
    step = row_chunk(ext)
    chunks = ext // step
    vmem = pl.BlockSpec(memory_space=pltpu.VMEM)
    dma = pltpu.SemaphoreType.DMA
    coarse = pl.pallas_call(
        functools.partial(image_kernel, n_kern, n_slab),
        out_shape=jax.ShapeDtypeStruct((n_kern, ext, block), f32),
        in_specs=[vmem, vmem, vmem, pl.BlockSpec(memory_space=pltpu.SMEM)],
        out_specs=vmem,
        scratch_shapes=[
            pltpu.VMEM((half, fields, 2, w, w), f32),
            pltpu.VMEM((cols, 4 * w), bf16),
            pltpu.VMEM((2 * w, rows), bf16),
            pltpu.VMEM((2 * w, rows), bf16),
            pltpu.VMEM((ext, 2 * w), bf16),
            pltpu.VMEM((n_kern, 2 * w, 2 * block), bf16),
            pltpu.VMEM((n_slab, piece, w), f32),
            pltpu.VMEM((n_slab - 1, piece, w), f32),
            pltpu.VMEM((n_kern, piece, w), f32),
            pltpu.VMEM((n_slab, piece, w), f32),
            pltpu.VMEM((chunks, fields * step, 2 * w), bf16),
            pltpu.VMEM((n_kern, ext, block), f32),
            pltpu.VMEM((n_kern, ext, block), f32),
            dma((half,)), dma((half,)),
            dma((n_slab - 1,)), dma((n_slab - 1,)),
            dma((n_kern - 1,)), dma((n_kern - 1,)),
            dma((n_slab - 1,)), dma((n_slab - 1,)),
            dma((n_kern,)), dma((n_kern,)),
        ],
        compiler_params=pltpu.CompilerParams(
            collective_id=0, has_side_effects=True, vmem_limit_bytes=34 * 2**20),
        name="coarse_image",
    )(layout, band_freqs.reshape(1, w), kernels, eigen_values)
    dh, dl = interpolation(cols, n)
    wide = cols + 2 * SIDE
    return pl.pallas_call(
        functools.partial(bake_kernel, fields * n_kern),
        out_shape=[jax.ShapeDtypeStruct((rows, cols), f32)] * 2,
        in_specs=[vmem, vmem, vmem, pl.BlockSpec(memory_space=pltpu.SMEM)],
        out_specs=[vmem, vmem],
        scratch_shapes=[
            pltpu.VMEM((2 * ext, COARSE), bf16),
            pltpu.VMEM((ext, wide), f32),
            pltpu.VMEM((ext, wide), f32),
            pltpu.VMEM((ext, wide), f32),
        ],
        compiler_params=pltpu.CompilerParams(vmem_limit_bytes=34 * 2**20),
        name="interpolate_bake",
    )(coarse, jnp.asarray(dh), jnp.asarray(dl), bake_rates)


def solution(mesh):
    return jax.shard_map(
        functools.partial(shards, mesh.shape["kern"], mesh.shape["slab"]),
        mesh=mesh,
        in_specs=(P("slab", "kern"), P(), P(None, "kern", None, None), P("kern"), P()),
        out_specs=(P("slab", "kern"), P("slab", "kern")),
        check_vma=False,
    )
```

```python
import functools
import math

import jax
import jax.numpy as jnp
import numpy as np
from jax import lax
from jax.experimental import pallas as pl
from jax.experimental.pallas import tpu as pltpu
from jax.sharding import PartitionSpec as P

BAND = 256
COARSE = 4 * BAND
HALO = 8
SIDE = 64
f32 = jnp.float32
bf16 = jnp.bfloat16


def trig(count, total):
    m = count & (total - 1)
    quarter = total // 4
    quad = (m + quarter // 2) >> (quarter.bit_length() - 1)
    rest = m - quad * quarter
    x = rest.astype(f32) * (2.0 * math.pi / total)
    y = x * x
    s = x * (1.0 + y * (-1.0 / 6 + y * (1.0 / 120 + y * (-1.0 / 5040 + y * (1.0 / 362880)))))
    c = 1.0 + y * (-0.5 + y * (1.0 / 24 + y * (-1.0 / 720 + y * (1.0 / 40320 + y * (-1.0 / 3628800)))))
    odd = (quad & 1) == 1
    cos = jnp.where(odd, s, c)
    sin = jnp.where(odd, c, s)
    cos = jnp.where(((quad + 1) & 2) == 2, -cos, cos)
    sin = jnp.where((quad & 2) == 2, -sin, sin)
    return cos, sin


def split(a):
    hi = a.astype(bf16)
    return hi, (a - hi.astype(f32)).astype(bf16)


def dot(a, b):
    return jnp.dot(a, b, preferred_element_type=f32)


def row_chunk(ext, most):
    return max(c for c in range(16, most + 1, 16) if ext % c == 0)


def image_kernel(
    n_kern, n_slab, layout_hbm, frow_ref, kern_hbm, eig_ref, out_ref,
    layout_ref, kern_ref, in_sem, kb, colw, rowt_h, rowt_l, rowb, ct, part, recv_a, recv_b, spec, rf, acc, recv_s,
    send_k, recv_k, send_a, rsem_a, send_b, rsem_b, send_c, rsem_c, send_s, rsem_s,
):
    layout_in = pltpu.make_async_copy(layout_hbm, layout_ref, in_sem.at[0])
    kern_in = pltpu.make_async_copy(kern_hbm, kern_ref, in_sem.at[1])
    kern_in.start()
    layout_in.start()
    rows, cols = layout_ref.shape
    n = cols * n_kern
    fields = kern_ref.shape[1]
    w = kern_ref.shape[2]
    half = n_kern // 2
    ext = rows + 2 * HALO
    piece = 2 * w // n_slab
    my_k = lax.axis_index("kern")
    my_s = lax.axis_index("slab")
    my_h = my_k // 2
    core = my_k % 2

    def slab_peer(d):
        return lax.rem(my_s + d, n_slab)

    def kern_peer(d):
        return lax.rem(my_k + d, n_kern)

    barrier = pltpu.get_barrier_semaphore()

    @pl.loop(1, n_slab)
    def _(d):
        pl.semaphore_signal(barrier, inc=1, device_id={"slab": slab_peer(d)}, device_id_type=pl.DeviceIdType.MESH)

    for d in range(1, n_kern):
        pl.semaphore_signal(barrier, inc=1, device_id={"kern": kern_peer(d)}, device_id_type=pl.DeviceIdType.MESH)

    kern_in.wait()
    for f in range(fields):
        weight = jnp.sqrt(jnp.full((1, w), eig_ref[f], f32))
        for c in range(2):
            kb[my_h, f, c] = kern_ref[c, f] * weight
    pl.semaphore_wait(barrier, n_slab - 1 + n_kern - 1)

    def kern_copy(d):
        return pltpu.make_async_remote_copy(
            src_ref=kb.at[my_h], dst_ref=kb.at[my_h],
            send_sem=send_k.at[d - 1], recv_sem=recv_k.at[d - 1],
            device_id={"kern": lax.rem(my_h + d, half) * 2 + core}, device_id_type=pl.DeviceIdType.MESH)

    for d in range(1, half):
        kern_copy(d).start()

    fcol = jnp.transpose(jnp.broadcast_to(frow_ref[...], (w, w)))[:, 0:1]
    pos = my_k * cols + lax.broadcasted_iota(jnp.int32, (cols, w), 0)
    cos, sin = trig(pos * frow_ref[...], n)
    ch, cl = split(cos)
    sh, sl = split(sin)
    colw[:, 0:w] = ch
    colw[:, w:2 * w] = sh
    colw[:, 2 * w:3 * w] = cl
    colw[:, 3 * w:4 * w] = sl
    pos = my_s * rows + lax.broadcasted_iota(jnp.int32, (w, rows), 1)
    cos, sin = trig(pos * fcol, n)
    ch, cl = split(cos)
    sh, sl = split(sin)
    rowt_h[0:w] = ch
    rowt_h[w:2 * w] = sh
    rowt_l[0:w] = cl
    rowt_l[w:2 * w] = sl
    layout_in.wait()
    x = (2 * layout_ref[...] - 1).astype(f32).astype(bf16)
    along = dot(x, colw[...])
    ah, al = split(along[:, :2 * w] + along[:, 2 * w:])
    both = dot(rowt_h[...], ah) + (dot(rowt_h[...], al) + dot(rowt_l[...], ah))
    re = (both[:w, :w] - both[w:, w:]) * (1.0 / n)
    im = (both[:w, w:] + both[w:, :w]) * (-1.0 / n)
    full = jnp.concatenate([re, im], 0)
    for i in range(n_slab):
        part[i] = full[i * piece:(i + 1) * piece]

    def copy_a(d):
        return pltpu.make_async_remote_copy(
            src_ref=part.at[slab_peer(d)], dst_ref=recv_a.at[d - 1],
            send_sem=send_a.at[d - 1], recv_sem=rsem_a.at[d - 1],
            device_id={"slab": slab_peer(d)}, device_id_type=pl.DeviceIdType.MESH)

    @pl.loop(1, n_slab)
    def _(d):
        copy_a(d).start()

    r = lax.broadcasted_iota(jnp.int32, (ext, w), 0)
    pos = my_s * rows + jnp.where(r < rows + HALO, r, r - ext)
    cos, sin = trig(pos * frow_ref[...], n)
    rowb[:, 0:w] = cos.astype(bf16)
    rowb[:, w:2 * w] = sin.astype(bf16)
    block = COARSE // n_kern
    for j in range(n_kern):
        pos = (n // COARSE) * (j * block + lax.broadcasted_iota(jnp.int32, (w, block), 1))
        cos, sin = trig(pos * fcol, n)
        ct[j, 0:w, 0:block] = cos.astype(bf16)
        ct[j, 0:w, block:2 * block] = sin.astype(bf16)
        ct[j, w:2 * w, 0:block] = (-sin).astype(bf16)
        ct[j, w:2 * w, block:2 * block] = cos.astype(bf16)

    @pl.loop(1, n_slab)
    def _(d):
        copy_a(d).wait()

    total = part[my_s]
    for d in range(1, n_slab):
        total = total + recv_a[d - 1]
    recv_b[my_k] = total

    def copy_b(d):
        return pltpu.make_async_remote_copy(
            src_ref=recv_b.at[my_k], dst_ref=recv_b.at[my_k],
            send_sem=send_b.at[d - 1], recv_sem=rsem_b.at[d - 1],
            device_id={"kern": kern_peer(d)}, device_id_type=pl.DeviceIdType.MESH)

    for d in range(1, n_kern):
        copy_b(d).start()
    for d in range(1, n_kern):
        copy_b(d).wait()
    total = recv_b[0]
    for k in range(1, n_kern):
        total = total + recv_b[k]
    spec[my_s] = total

    def copy_c(d):
        return pltpu.make_async_remote_copy(
            src_ref=spec.at[my_s], dst_ref=spec.at[my_s],
            send_sem=send_c.at[d - 1], recv_sem=rsem_c.at[d - 1],
            device_id={"slab": slab_peer(d)}, device_id_type=pl.DeviceIdType.MESH)

    @pl.loop(1, n_slab)
    def _(d):
        copy_c(d).start()

    @pl.loop(1, n_slab)
    def _(d):
        copy_c(d).wait()

    full = jnp.concatenate([spec[i] for i in range(n_slab)], 0)
    spec_re = full[:w]
    spec_im = full[w:]
    step = row_chunk(ext, 192)
    chunks = ext // step
    partner = my_k + 1 - 2 * core

    def copy_s(j):
        return pltpu.make_async_remote_copy(
            src_ref=acc.at[j], dst_ref=recv_s.at[j],
            send_sem=send_s.at[j], recv_sem=rsem_s.at[j],
            device_id={"kern": partner}, device_id_type=pl.DeviceIdType.MESH)

    for phase in range(half):
        h = lax.rem(my_h + half - phase, half)
        if phase > 0:
            kern_copy(phase).wait()

        @pl.loop(0, fields, unroll=3)
        def _(f):
            kr = kb[h, f, 0]
            ki = kb[h, f, 1]
            pr = spec_re * kr - spec_im * ki
            pi = spec_re * ki + spec_im * kr
            prod = jnp.concatenate(
                [jnp.concatenate([pr, pi], 1), jnp.concatenate([-pi, pr], 1)], 0).astype(bf16)
            field = (dot(rowb[...], prod) * (1.0 / w)).astype(bf16)
            at = pl.multiple_of(f * step, 16)
            for i in range(chunks):
                rf[i, pl.ds(at, step), :] = field[i * step:(i + 1) * step]

        @pl.loop(0, n_kern)
        def _(j):
            @pl.loop(0, chunks)
            def _(i):
                at = pl.ds(pl.multiple_of(i * step, 16), step)
                e = dot(rf[i], ct[j])
                total = None if phase == 0 else acc[j, at, :]
                for f in range(fields):
                    one = e[f * step:(f + 1) * step]
                    sq = one * one
                    sq = sq[:, :block] + sq[:, block:]
                    total = sq if total is None else total + sq
                acc[j, at, :] = total

            if phase == half - 1:
                copy_s(j).start()

    for j in range(n_kern):
        copy_s(j).wait()
        out_ref[lax.rem(j + n_kern - my_k, n_kern)] = acc[j] + recv_s[j]


def bake_kernel(fields, coarse_ref, dh_ref, dl_ref, rates_ref, aer_ref, lat_ref, xs, aer, acid0, acid1):
    n_kern, ext, block = coarse_ref.shape
    rows, cols = aer_ref.shape
    wide = dh_ref.shape[1]
    step = row_chunk(ext, 96)
    chunks = ext // step
    dill, arate, react, qstart = rates_ref[0], rates_ref[1], rates_ref[3], rates_ref[4]
    for j in range(n_kern):
        hi, lo = split(coarse_ref[j])
        xs[0:ext, j * block:(j + 1) * block] = hi
        xs[ext:2 * ext, j * block:(j + 1) * block] = lo
    tile = 384 if wide % 384 == 0 else 128
    for c in range(0, wide, tile):
        s = slice(c, c + tile)
        both = dot(xs[...], dh_ref[:, s])
        value = (both[:ext] + (both[ext:] + dot(xs[0:ext, :], dl_ref[:, s]))) * (1.0 / fields)
        aer[:, s] = value
        acid0[:, s] = 1.0 - jnp.exp((-4.0 * dill) * value)

    aer_ref[...] = aer[0:rows, 0:cols]

    def laplace(ref, i):
        first = i * step
        mid = ref[pl.ds(pl.multiple_of(first, 8), step), :]
        before = ref[pl.ds(pl.multiple_of(lax.rem(first + ext - 8, ext), 8), 8), :]
        after = ref[pl.ds(pl.multiple_of(lax.rem(first + step, ext), 8), 8), :]
        tall = jnp.concatenate([before, mid, after], 0)
        up = pltpu.roll(tall, 1, 0)[8:8 + step]
        down = pltpu.roll(tall, step + 15, 0)[8:8 + step]
        left = pltpu.roll(mid, 1, 1)
        right = pltpu.roll(mid, wide - 1, 1)
        return mid, down + up + right + left - 4.0 * mid

    @pl.loop(0, chunks)
    def _(i):
        mid, lap = laplace(acid0, i)
        value = mid + (arate * (0.5 + 0.5 * mid)) * lap - 4.0 * react * mid * qstart
        acid1[pl.ds(pl.multiple_of(i * step, 16), step), :] = value

    @pl.loop(0, chunks)
    def _(i):
        at = pl.ds(pl.multiple_of(i * step, 16), step)
        mid, lap = laplace(acid1, i)
        first = acid0[at, :]
        quench = qstart - 4.0 * react * first * qstart
        aer[at, :] = mid + (arate * (0.5 + 0.5 * first)) * lap - 4.0 * react * mid * quench

    lat_ref[...] = aer[0:rows, 0:cols]


def interpolation(cols, n):
    wide = cols + 2 * SIDE
    c = np.arange(wide)
    c = np.where(c < cols + SIDE, c, c - wide)
    ratio = n // COARSE
    t = c[None, :] - ratio * np.arange(COARSE)[:, None]
    zero = t % n == 0
    safe = np.where(zero, 1, t)
    d = np.sin(np.pi * (safe % (2 * ratio)) / ratio) / (COARSE * np.tan(np.pi * safe / n))
    d = np.where(zero, 1.0, np.where(t % ratio == 0, 0.0, d))
    hi = d.astype(jnp.bfloat16)
    lo = (d - hi.astype(np.float64)).astype(jnp.bfloat16)
    return hi, lo


def shards(n_kern, n_slab, layout, band_freqs, kernels, eigen_values, bake_rates):
    rows, cols = layout.shape
    fields, w = kernels.shape[1], kernels.shape[2]
    n = cols * n_kern
    ext = rows + 2 * HALO
    half = n_kern // 2
    block = COARSE // n_kern
    piece = 2 * w // n_slab
    step = row_chunk(ext, 192)
    chunks = ext // step
    vmem = pl.BlockSpec(memory_space=pltpu.VMEM)
    anyw = pl.BlockSpec(memory_space=pl.ANY)
    dma = pltpu.SemaphoreType.DMA
    coarse = pl.pallas_call(
        functools.partial(image_kernel, n_kern, n_slab),
        out_shape=jax.ShapeDtypeStruct((n_kern, ext, block), f32),
        in_specs=[anyw, vmem, anyw, pl.BlockSpec(memory_space=pltpu.SMEM)],
        out_specs=vmem,
        scratch_shapes=[
            pltpu.VMEM((rows, cols), jnp.int32),
            pltpu.VMEM((2, fields, w, w), f32),
            dma((2,)),
            pltpu.VMEM((half, fields, 2, w, w), f32),
            pltpu.VMEM((cols, 4 * w), bf16),
            pltpu.VMEM((2 * w, rows), bf16),
            pltpu.VMEM((2 * w, rows), bf16),
            pltpu.VMEM((ext, 2 * w), bf16),
            pltpu.VMEM((n_kern, 2 * w, 2 * block), bf16),
            pltpu.VMEM((n_slab, piece, w), f32),
            pltpu.VMEM((n_slab - 1, piece, w), f32),
            pltpu.VMEM((n_kern, piece, w), f32),
            pltpu.VMEM((n_slab, piece, w), f32),
            pltpu.VMEM((chunks, fields * step, 2 * w), bf16),
            pltpu.VMEM((n_kern, ext, block), f32),
            pltpu.VMEM((n_kern, ext, block), f32),
            dma((half,)), dma((half,)),
            dma((n_slab - 1,)), dma((n_slab - 1,)),
            dma((n_kern - 1,)), dma((n_kern - 1,)),
            dma((n_slab - 1,)), dma((n_slab - 1,)),
            dma((n_kern,)), dma((n_kern,)),
        ],
        compiler_params=pltpu.CompilerParams(
            collective_id=0, has_side_effects=True, vmem_limit_bytes=56 * 2**20),
        name="coarse_image",
    )(layout, band_freqs.reshape(1, w), kernels, eigen_values)
    dh, dl = interpolation(cols, n)
    wide = cols + 2 * SIDE
    return pl.pallas_call(
        functools.partial(bake_kernel, fields * n_kern),
        out_shape=[jax.ShapeDtypeStruct((rows, cols), f32)] * 2,
        in_specs=[vmem, vmem, vmem, pl.BlockSpec(memory_space=pltpu.SMEM)],
        out_specs=[vmem, vmem],
        scratch_shapes=[
            pltpu.VMEM((2 * ext, COARSE), bf16),
            pltpu.VMEM((ext, wide), f32),
            pltpu.VMEM((ext, wide), f32),
            pltpu.VMEM((ext, wide), f32),
        ],
        compiler_params=pltpu.CompilerParams(vmem_limit_bytes=34 * 2**20),
        name="interpolate_bake",
    )(coarse, jnp.asarray(dh), jnp.asarray(dl), bake_rates)


def solution(mesh):
    return jax.shard_map(
        functools.partial(shards, mesh.shape["kern"], mesh.shape["slab"]),
        mesh=mesh,
        in_specs=(P("slab", "kern"), P(), P(None, "kern", None, None), P("kern"), P()),
        out_specs=(P("slab", "kern"), P("slab", "kern")),
        check_vma=False,
    )
```

```python
import functools
import math

import jax
import jax.numpy as jnp
import numpy as np
from jax import lax
from jax.experimental import pallas as pl
from jax.experimental.pallas import tpu as pltpu
from jax.sharding import PartitionSpec as P

BAND = 256
COARSE = 4 * BAND
HALO = 8
SIDE = 64
f32 = jnp.float32
bf16 = jnp.bfloat16


def trig(count, total):
    m = count & (total - 1)
    quarter = total // 4
    quad = (m + quarter // 2) >> (quarter.bit_length() - 1)
    rest = m - quad * quarter
    x = rest.astype(f32) * (2.0 * math.pi / total)
    y = x * x
    s = x * (1.0 + y * (-1.0 / 6 + y * (1.0 / 120 + y * (-1.0 / 5040 + y * (1.0 / 362880)))))
    c = 1.0 + y * (-0.5 + y * (1.0 / 24 + y * (-1.0 / 720 + y * (1.0 / 40320 + y * (-1.0 / 3628800)))))
    odd = (quad & 1) == 1
    cos = jnp.where(odd, s, c)
    sin = jnp.where(odd, c, s)
    cos = jnp.where(((quad + 1) & 2) == 2, -cos, cos)
    sin = jnp.where((quad & 2) == 2, -sin, sin)
    return cos, sin


def split(a):
    hi = a.astype(bf16)
    return hi, (a - hi.astype(f32)).astype(bf16)


def dot(a, b):
    return jnp.dot(a, b, preferred_element_type=f32)


def row_chunk(ext, most):
    return max(c for c in range(16, most + 1, 16) if ext % c == 0)


def image_kernel(
    n_kern, n_slab, layout_hbm, frow_ref, kern_hbm, eig_ref, out_ref,
    layout_ref, kern_ref, in_sem, kb, colw, rowt_h, rowt_l, rowb, ct, part, recv_a, recv_b, spec, rf, acc, recv_s,
    send_k, recv_k, send_a, rsem_a, send_b, rsem_b, send_c, rsem_c, send_s, rsem_s,
):
    layout_in = pltpu.make_async_copy(layout_hbm, layout_ref, in_sem.at[0])
    kern_in = pltpu.make_async_copy(kern_hbm, kern_ref, in_sem.at[1])
    kern_in.start()
    layout_in.start()
    rows, cols = layout_ref.shape
    n = cols * n_kern
    fields = kern_ref.shape[1]
    w = kern_ref.shape[2]
    half = n_kern // 2
    ext = rows + 2 * HALO
    piece = 2 * w // n_slab
    my_k = lax.axis_index("kern")
    my_s = lax.axis_index("slab")
    my_h = my_k // 2
    core = my_k % 2

    def slab_peer(d):
        return lax.rem(my_s + d, n_slab)

    def kern_peer(d):
        return lax.rem(my_k + d, n_kern)

    barrier = pltpu.get_barrier_semaphore()

    @pl.loop(1, n_slab)
    def _(d):
        pl.semaphore_signal(barrier, inc=1, device_id={"slab": slab_peer(d)}, device_id_type=pl.DeviceIdType.MESH)

    for d in range(1, n_kern):
        pl.semaphore_signal(barrier, inc=1, device_id={"kern": kern_peer(d)}, device_id_type=pl.DeviceIdType.MESH)

    kern_in.wait()
    for f in range(fields):
        weight = jnp.sqrt(jnp.full((1, w), eig_ref[f], f32))
        for c in range(2):
            kb[my_h, f, c] = kern_ref[c, f] * weight
    pl.semaphore_wait(barrier, n_slab - 1 + n_kern - 1)

    early = fields // 4

    def kern_copy(d, late):
        some = pl.ds(early, fields - early) if late else pl.ds(0, early)
        return pltpu.make_async_remote_copy(
            src_ref=kb.at[my_h, some], dst_ref=kb.at[my_h, some],
            send_sem=send_k.at[late, d - 1], recv_sem=recv_k.at[late, d - 1],
            device_id={"kern": lax.rem(my_h + d, half) * 2 + core}, device_id_type=pl.DeviceIdType.MESH)

    for d in range(1, half):
        kern_copy(d, 0).start()

    fcol = jnp.transpose(jnp.broadcast_to(frow_ref[...], (w, w)))[:, 0:1]
    pos = my_k * cols + lax.broadcasted_iota(jnp.int32, (cols, w), 0)
    cos, sin = trig(pos * frow_ref[...], n)
    ch, cl = split(cos)
    sh, sl = split(sin)
    colw[:, 0:w] = ch
    colw[:, w:2 * w] = sh
    colw[:, 2 * w:3 * w] = cl
    colw[:, 3 * w:4 * w] = sl
    pos = my_s * rows + lax.broadcasted_iota(jnp.int32, (w, rows), 1)
    cos, sin = trig(pos * fcol, n)
    ch, cl = split(cos)
    sh, sl = split(sin)
    rowt_h[0:w] = ch
    rowt_h[w:2 * w] = sh
    rowt_l[0:w] = cl
    rowt_l[w:2 * w] = sl
    layout_in.wait()
    x = (2 * layout_ref[...] - 1).astype(f32).astype(bf16)
    along = dot(x, colw[...])
    ah, al = split(along[:, :2 * w] + along[:, 2 * w:])
    both = dot(rowt_h[...], ah) + (dot(rowt_h[...], al) + dot(rowt_l[...], ah))
    re = (both[:w, :w] - both[w:, w:]) * (1.0 / n)
    im = (both[:w, w:] + both[w:, :w]) * (-1.0 / n)
    full = jnp.concatenate([re, im], 0)
    for i in range(n_slab):
        part[i] = full[i * piece:(i + 1) * piece]

    def copy_a(d):
        return pltpu.make_async_remote_copy(
            src_ref=part.at[slab_peer(d)], dst_ref=recv_a.at[d - 1],
            send_sem=send_a.at[d - 1], recv_sem=rsem_a.at[d - 1],
            device_id={"slab": slab_peer(d)}, device_id_type=pl.DeviceIdType.MESH)

    @pl.loop(1, n_slab)
    def _(d):
        copy_a(d).start()

    r = lax.broadcasted_iota(jnp.int32, (ext, w), 0)
    pos = my_s * rows + jnp.where(r < rows + HALO, r, r - ext)
    cos, sin = trig(pos * frow_ref[...], n)
    rowb[:, 0:w] = cos.astype(bf16)
    rowb[:, w:2 * w] = sin.astype(bf16)
    block = COARSE // n_kern
    for j in range(n_kern):
        pos = (n // COARSE) * (j * block + lax.broadcasted_iota(jnp.int32, (w, block), 1))
        cos, sin = trig(pos * fcol, n)
        ct[j, 0:w, 0:block] = cos.astype(bf16)
        ct[j, 0:w, block:2 * block] = sin.astype(bf16)
        ct[j, w:2 * w, 0:block] = (-sin).astype(bf16)
        ct[j, w:2 * w, block:2 * block] = cos.astype(bf16)

    @pl.loop(1, n_slab)
    def _(d):
        copy_a(d).wait()

    total = part[my_s]
    for d in range(1, n_slab):
        total = total + recv_a[d - 1]
    recv_b[my_k] = total

    def copy_b(d):
        return pltpu.make_async_remote_copy(
            src_ref=recv_b.at[my_k], dst_ref=recv_b.at[my_k],
            send_sem=send_b.at[d - 1], recv_sem=rsem_b.at[d - 1],
            device_id={"kern": kern_peer(d)}, device_id_type=pl.DeviceIdType.MESH)

    for d in range(1, n_kern):
        copy_b(d).start()
    for d in range(1, n_kern):
        copy_b(d).wait()
    for d in range(1, half):
        kern_copy(d, 1).start()
    total = recv_b[0]
    for k in range(1, n_kern):
        total = total + recv_b[k]
    spec[my_s] = total

    def copy_c(d):
        return pltpu.make_async_remote_copy(
            src_ref=spec.at[my_s], dst_ref=spec.at[my_s],
            send_sem=send_c.at[d - 1], recv_sem=rsem_c.at[d - 1],
            device_id={"slab": slab_peer(d)}, device_id_type=pl.DeviceIdType.MESH)

    @pl.loop(1, n_slab)
    def _(d):
        copy_c(d).start()

    @pl.loop(1, n_slab)
    def _(d):
        copy_c(d).wait()

    full = jnp.concatenate([spec[i] for i in range(n_slab)], 0)
    spec_re = full[:w]
    spec_im = full[w:]
    step = row_chunk(ext, 192)
    chunks = ext // step
    partner = my_k + 1 - 2 * core

    def copy_s(j):
        return pltpu.make_async_remote_copy(
            src_ref=acc.at[j], dst_ref=recv_s.at[j],
            send_sem=send_s.at[j], recv_sem=rsem_s.at[j],
            device_id={"kern": partner}, device_id_type=pl.DeviceIdType.MESH)

    for phase in range(half):
        h = lax.rem(my_h + half - phase, half)
        if phase > 0:
            kern_copy(phase, 0).wait()
            kern_copy(phase, 1).wait()

        @pl.loop(0, fields, unroll=3)
        def _(f):
            kr = kb[h, f, 0]
            ki = kb[h, f, 1]
            pr = spec_re * kr - spec_im * ki
            pi = spec_re * ki + spec_im * kr
            prod = jnp.concatenate(
                [jnp.concatenate([pr, pi], 1), jnp.concatenate([-pi, pr], 1)], 0).astype(bf16)
            field = (dot(rowb[...], prod) * (1.0 / w)).astype(bf16)
            at = pl.multiple_of(f * step, 16)
            for i in range(chunks):
                rf[i, pl.ds(at, step), :] = field[i * step:(i + 1) * step]

        @pl.loop(0, n_kern)
        def _(j):
            @pl.loop(0, chunks)
            def _(i):
                at = pl.ds(pl.multiple_of(i * step, 16), step)
                e = dot(rf[i], ct[j])
                total = None if phase == 0 else acc[j, at, :]
                for f in range(fields):
                    one = e[f * step:(f + 1) * step]
                    sq = one * one
                    sq = sq[:, :block] + sq[:, block:]
                    total = sq if total is None else total + sq
                acc[j, at, :] = total

            if phase == half - 1:
                copy_s(j).start()

    for j in range(n_kern):
        copy_s(j).wait()
        out_ref[lax.rem(j + n_kern - my_k, n_kern)] = acc[j] + recv_s[j]


def bake_kernel(fields, coarse_ref, dh_ref, dl_ref, rates_ref, aer_hbm, lat_hbm, xs, aer, acid0, acid1, lat, sem):
    n_kern, ext, block = coarse_ref.shape
    rows, cols = aer_hbm.shape
    wide = dh_ref.shape[1]
    step = row_chunk(ext, 96)
    chunks = ext // step
    dill, arate, react, qstart = rates_ref[0], rates_ref[1], rates_ref[3], rates_ref[4]
    for j in range(n_kern):
        hi, lo = split(coarse_ref[j])
        xs[0:ext, j * block:(j + 1) * block] = hi
        xs[ext:2 * ext, j * block:(j + 1) * block] = lo
    tile = 384 if wide % 384 == 0 else 128
    for c in range(0, wide, tile):
        s = slice(c, c + tile)
        both = dot(xs[...], dh_ref[:, s])
        value = (both[:ext] + (both[ext:] + dot(xs[0:ext, :], dl_ref[:, s]))) * (1.0 / fields)
        aer[:, s] = value
        acid0[:, s] = 1.0 - jnp.exp((-4.0 * dill) * value)

    aer_out = pltpu.make_async_copy(aer.at[0:rows, 0:cols], aer_hbm, sem.at[0])
    aer_out.start()

    def laplace(ref, first, step):
        mid = ref[pl.ds(pl.multiple_of(first, 8), step), :]
        before = ref[pl.ds(pl.multiple_of(lax.rem(first + ext - 8, ext), 8), 8), :]
        after = ref[pl.ds(pl.multiple_of(lax.rem(first + step, ext), 8), 8), :]
        tall = jnp.concatenate([before, mid, after], 0)
        up = pltpu.roll(tall, 1, 0)[8:8 + step]
        down = pltpu.roll(tall, step + 15, 0)[8:8 + step]
        left = pltpu.roll(mid, 1, 1)
        right = pltpu.roll(mid, wide - 1, 1)
        return mid, down + up + right + left - 4.0 * mid

    @pl.loop(0, chunks)
    def _(i):
        mid, lap = laplace(acid0, i * step, step)
        value = mid + (arate * (0.5 + 0.5 * mid)) * lap - 4.0 * react * mid * qstart
        acid1[pl.ds(pl.multiple_of(i * step, 16), step), :] = value

    last = math.gcd(rows, 64)
    parts = rows // last

    def lat_out(i):
        at = pl.ds(pl.multiple_of(i * last, 16), last)
        return pltpu.make_async_copy(lat.at[at, :], lat_hbm.at[at, :], sem.at[1 + i])

    @pl.loop(0, parts)
    def _(i):
        at = pl.ds(pl.multiple_of(i * last, 16), last)
        mid, lap = laplace(acid1, i * last, last)
        first = acid0[at, :]
        quench = qstart - 4.0 * react * first * qstart
        value = mid + (arate * (0.5 + 0.5 * first)) * lap - 4.0 * react * mid * quench
        lat[at, :] = value[:, 0:cols]
        lat_out(i).start()

    aer_out.wait()

    @pl.loop(0, parts)
    def _(i):
        lat_out(i).wait()


def interpolation(cols, n):
    wide = cols + 2 * SIDE
    c = np.arange(wide)
    c = np.where(c < cols + SIDE, c, c - wide)
    ratio = n // COARSE
    t = c[None, :] - ratio * np.arange(COARSE)[:, None]
    zero = t % n == 0
    safe = np.where(zero, 1, t)
    d = np.sin(np.pi * (safe % (2 * ratio)) / ratio) / (COARSE * np.tan(np.pi * safe / n))
    d = np.where(zero, 1.0, np.where(t % ratio == 0, 0.0, d))
    hi = d.astype(jnp.bfloat16)
    lo = (d - hi.astype(np.float64)).astype(jnp.bfloat16)
    return hi, lo


def shards(n_kern, n_slab, layout, band_freqs, kernels, eigen_values, bake_rates):
    rows, cols = layout.shape
    fields, w = kernels.shape[1], kernels.shape[2]
    n = cols * n_kern
    ext = rows + 2 * HALO
    half = n_kern // 2
    block = COARSE // n_kern
    piece = 2 * w // n_slab
    step = row_chunk(ext, 192)
    chunks = ext // step
    vmem = pl.BlockSpec(memory_space=pltpu.VMEM)
    anyw = pl.BlockSpec(memory_space=pl.ANY)
    dma = pltpu.SemaphoreType.DMA
    coarse = pl.pallas_call(
        functools.partial(image_kernel, n_kern, n_slab),
        out_shape=jax.ShapeDtypeStruct((n_kern, ext, block), f32),
        in_specs=[anyw, vmem, anyw, pl.BlockSpec(memory_space=pltpu.SMEM)],
        out_specs=vmem,
        scratch_shapes=[
            pltpu.VMEM((rows, cols), jnp.int32),
            pltpu.VMEM((2, fields, w, w), f32),
            dma((2,)),
            pltpu.VMEM((half, fields, 2, w, w), f32),
            pltpu.VMEM((cols, 4 * w), bf16),
            pltpu.VMEM((2 * w, rows), bf16),
            pltpu.VMEM((2 * w, rows), bf16),
            pltpu.VMEM((ext, 2 * w), bf16),
            pltpu.VMEM((n_kern, 2 * w, 2 * block), bf16),
            pltpu.VMEM((n_slab, piece, w), f32),
            pltpu.VMEM((n_slab - 1, piece, w), f32),
            pltpu.VMEM((n_kern, piece, w), f32),
            pltpu.VMEM((n_slab, piece, w), f32),
            pltpu.VMEM((chunks, fields * step, 2 * w), bf16),
            pltpu.VMEM((n_kern, ext, block), f32),
            pltpu.VMEM((n_kern, ext, block), f32),
            dma((2, half)), dma((2, half)),
            dma((n_slab - 1,)), dma((n_slab - 1,)),
            dma((n_kern - 1,)), dma((n_kern - 1,)),
            dma((n_slab - 1,)), dma((n_slab - 1,)),
            dma((n_kern,)), dma((n_kern,)),
        ],
        compiler_params=pltpu.CompilerParams(
            collective_id=0, has_side_effects=True, vmem_limit_bytes=56 * 2**20),
        name="coarse_image",
    )(layout, band_freqs.reshape(1, w), kernels, eigen_values)
    dh, dl = interpolation(cols, n)
    wide = cols + 2 * SIDE
    return pl.pallas_call(
        functools.partial(bake_kernel, fields * n_kern),
        out_shape=[jax.ShapeDtypeStruct((rows, cols), f32)] * 2,
        in_specs=[vmem, vmem, vmem, pl.BlockSpec(memory_space=pltpu.SMEM)],
        out_specs=[anyw, anyw],
        scratch_shapes=[
            pltpu.VMEM((2 * ext, COARSE), bf16),
            pltpu.VMEM((ext, wide), f32),
            pltpu.VMEM((ext, wide), f32),
            pltpu.VMEM((ext, wide), f32),
            pltpu.VMEM((rows, cols), f32),
            dma((1 + rows // math.gcd(rows, 64),)),
        ],
        compiler_params=pltpu.CompilerParams(vmem_limit_bytes=34 * 2**20),
        name="interpolate_bake",
    )(coarse, jnp.asarray(dh), jnp.asarray(dl), bake_rates)


def solution(mesh):
    return jax.shard_map(
        functools.partial(shards, mesh.shape["kern"], mesh.shape["slab"]),
        mesh=mesh,
        in_specs=(P("slab", "kern"), P(), P(None, "kern", None, None), P("kern"), P()),
        out_specs=(P("slab", "kern"), P("slab", "kern")),
        check_vma=False,
    )
```

```python
import functools
import math

import jax
import jax.numpy as jnp
import numpy as np
from jax import lax
from jax.experimental import pallas as pl
from jax.experimental.pallas import tpu as pltpu
from jax.sharding import PartitionSpec as P

BAND = 256
COARSE = 4 * BAND
HALO = 8
SIDE = 64
f32 = jnp.float32
bf16 = jnp.bfloat16


def trig(count, total):
    m = count & (total - 1)
    quarter = total // 4
    quad = (m + quarter // 2) >> (quarter.bit_length() - 1)
    rest = m - quad * quarter
    x = rest.astype(f32) * (2.0 * math.pi / total)
    y = x * x
    s = x * (1.0 + y * (-1.0 / 6 + y * (1.0 / 120 + y * (-1.0 / 5040 + y * (1.0 / 362880)))))
    c = 1.0 + y * (-0.5 + y * (1.0 / 24 + y * (-1.0 / 720 + y * (1.0 / 40320 + y * (-1.0 / 3628800)))))
    odd = (quad & 1) == 1
    cos = jnp.where(odd, s, c)
    sin = jnp.where(odd, c, s)
    cos = jnp.where(((quad + 1) & 2) == 2, -cos, cos)
    sin = jnp.where((quad & 2) == 2, -sin, sin)
    return cos, sin


def split(a):
    hi = a.astype(bf16)
    return hi, (a - hi.astype(f32)).astype(bf16)


def dot(a, b):
    return jnp.dot(a, b, preferred_element_type=f32)


def row_chunk(ext, most):
    return max(c for c in range(16, most + 1, 16) if ext % c == 0)


def image_kernel(
    n_kern, n_slab, layout_hbm, frow_ref, kern_hbm, eig_ref, out_ref,
    layout_ref, kern_ref, in_sem, kb, colw, rowt_h, rowt_l, rowb, ct, part, recv_a, recv_b, spec, rf, acc, recv_s,
    send_k, recv_k, send_a, rsem_a, send_b, rsem_b, send_c, rsem_c, send_s, rsem_s,
):
    layout_in = pltpu.make_async_copy(layout_hbm, layout_ref, in_sem.at[0])
    kern_in = pltpu.make_async_copy(kern_hbm, kern_ref, in_sem.at[1])
    kern_in.start()
    layout_in.start()
    rows, cols = layout_ref.shape
    n = cols * n_kern
    fields = kern_ref.shape[1]
    w = kern_ref.shape[2]
    half = n_kern // 2
    ext = rows + 2 * HALO
    piece = 2 * w // n_slab
    my_k = lax.axis_index("kern")
    my_s = lax.axis_index("slab")
    my_h = my_k // 2
    core = my_k % 2

    def slab_peer(d):
        return lax.rem(my_s + d, n_slab)

    def kern_peer(d):
        return lax.rem(my_k + d, n_kern)

    barrier = pltpu.get_barrier_semaphore()

    @pl.loop(1, n_slab)
    def _(d):
        pl.semaphore_signal(barrier, inc=1, device_id={"slab": slab_peer(d)}, device_id_type=pl.DeviceIdType.MESH)

    for d in range(1, n_kern):
        pl.semaphore_signal(barrier, inc=1, device_id={"kern": kern_peer(d)}, device_id_type=pl.DeviceIdType.MESH)

    kern_in.wait()
    for f in range(fields):
        weight = jnp.sqrt(jnp.full((1, w), eig_ref[f], f32))
        for c in range(2):
            kb[my_h, f, c] = kern_ref[c, f] * weight

    early = fields // 3

    def kern_copy(d, late):
        some = pl.ds(early, fields - early) if late else pl.ds(0, early)
        return pltpu.make_async_remote_copy(
            src_ref=kb.at[my_h, some], dst_ref=kb.at[my_h, some],
            send_sem=send_k.at[late, d - 1], recv_sem=recv_k.at[late, d - 1],
            device_id={"kern": lax.rem(my_h + d, half) * 2 + core}, device_id_type=pl.DeviceIdType.MESH)

    fcol = jnp.transpose(jnp.broadcast_to(frow_ref[...], (w, w)))[:, 0:1]
    pos = my_k * cols + lax.broadcasted_iota(jnp.int32, (cols, w), 0)
    cos, sin = trig(pos * frow_ref[...], n)
    ch, cl = split(cos)
    sh, sl = split(sin)
    colw[:, 0:w] = ch
    colw[:, w:2 * w] = sh
    colw[:, 2 * w:3 * w] = cl
    colw[:, 3 * w:4 * w] = sl
    pl.semaphore_wait(barrier, n_slab - 1 + n_kern - 1)
    for d in range(1, half):
        kern_copy(d, 0).start()
    pos = my_s * rows + lax.broadcasted_iota(jnp.int32, (w, rows), 1)
    cos, sin = trig(pos * fcol, n)
    ch, cl = split(cos)
    sh, sl = split(sin)
    rowt_h[0:w] = ch
    rowt_h[w:2 * w] = sh
    rowt_l[0:w] = cl
    rowt_l[w:2 * w] = sl
    layout_in.wait()
    x = (2 * layout_ref[...] - 1).astype(f32).astype(bf16)
    along = dot(x, colw[...])
    ah, al = split(along[:, :2 * w] + along[:, 2 * w:])
    both = dot(rowt_h[...], ah) + (dot(rowt_h[...], al) + dot(rowt_l[...], ah))
    re = (both[:w, :w] - both[w:, w:]) * (1.0 / n)
    im = (both[:w, w:] + both[w:, :w]) * (-1.0 / n)
    full = jnp.concatenate([re, im], 0)
    for i in range(n_slab):
        part[i] = full[i * piece:(i + 1) * piece]

    def copy_a(d):
        return pltpu.make_async_remote_copy(
            src_ref=part.at[slab_peer(d)], dst_ref=recv_a.at[d - 1],
            send_sem=send_a.at[d - 1], recv_sem=rsem_a.at[d - 1],
            device_id={"slab": slab_peer(d)}, device_id_type=pl.DeviceIdType.MESH)

    @pl.loop(1, n_slab)
    def _(d):
        copy_a(d).start()

    r = lax.broadcasted_iota(jnp.int32, (ext, w), 0)
    pos = my_s * rows + jnp.where(r < rows + HALO, r, r - ext)
    cos, sin = trig(pos * frow_ref[...], n)
    rowb[:, 0:w] = cos.astype(bf16)
    rowb[:, w:2 * w] = sin.astype(bf16)
    block = COARSE // n_kern
    for j in range(n_kern):
        pos = (n // COARSE) * (j * block + lax.broadcasted_iota(jnp.int32, (w, block), 1))
        cos, sin = trig(pos * fcol, n)
        ct[j, 0:w, 0:block] = cos.astype(bf16)
        ct[j, 0:w, block:2 * block] = sin.astype(bf16)
        ct[j, w:2 * w, 0:block] = (-sin).astype(bf16)
        ct[j, w:2 * w, block:2 * block] = cos.astype(bf16)

    @pl.loop(1, n_slab)
    def _(d):
        copy_a(d).wait()

    total = part[my_s]
    for d in range(1, n_slab):
        total = total + recv_a[d - 1]
    recv_b[my_k] = total

    def copy_b(d):
        return pltpu.make_async_remote_copy(
            src_ref=recv_b.at[my_k], dst_ref=recv_b.at[my_k],
            send_sem=send_b.at[d - 1], recv_sem=rsem_b.at[d - 1],
            device_id={"kern": kern_peer(d)}, device_id_type=pl.DeviceIdType.MESH)

    for d in range(1, n_kern):
        copy_b(d).start()
    for d in range(1, n_kern):
        copy_b(d).wait()
    for d in range(1, half):
        kern_copy(d, 1).start()
    total = recv_b[0]
    for k in range(1, n_kern):
        total = total + recv_b[k]
    spec[my_s] = total

    def copy_c(d):
        return pltpu.make_async_remote_copy(
            src_ref=spec.at[my_s], dst_ref=spec.at[my_s],
            send_sem=send_c.at[d - 1], recv_sem=rsem_c.at[d - 1],
            device_id={"slab": slab_peer(d)}, device_id_type=pl.DeviceIdType.MESH)

    @pl.loop(1, n_slab)
    def _(d):
        copy_c(d).start()

    @pl.loop(1, n_slab)
    def _(d):
        copy_c(d).wait()

    full = jnp.concatenate([spec[i] for i in range(n_slab)], 0)
    spec_re = full[:w]
    spec_im = full[w:]
    step = row_chunk(ext, 192)
    chunks = ext // step
    partner = my_k + 1 - 2 * core

    def copy_s(j):
        return pltpu.make_async_remote_copy(
            src_ref=acc.at[j], dst_ref=recv_s.at[j],
            send_sem=send_s.at[j], recv_sem=rsem_s.at[j],
            device_id={"kern": partner}, device_id_type=pl.DeviceIdType.MESH)

    groups = [(0, 0, fields)]
    for phase in range(1, half):
        groups += [(phase, 0, early), (phase, early, fields - early)]
    for phase, first, some in groups:
        h = lax.rem(my_h + half - phase, half)
        if phase > 0:
            kern_copy(phase, int(first > 0)).wait()

        @pl.loop(0, some, unroll=4)
        def _(f):
            kr = kb[h, first + f, 0]
            ki = kb[h, first + f, 1]
            pr = spec_re * kr - spec_im * ki
            pi = spec_re * ki + spec_im * kr
            prod = jnp.concatenate(
                [jnp.concatenate([pr, pi], 1), jnp.concatenate([-pi, pr], 1)], 0).astype(bf16)
            field = (dot(rowb[...], prod) * (1.0 / w)).astype(bf16)
            at = pl.multiple_of(f * step, 16)
            for i in range(chunks):
                rf[i, pl.ds(at, step), :] = field[i * step:(i + 1) * step]

        @pl.loop(0, n_kern)
        def _(j):
            @pl.loop(0, chunks)
            def _(i):
                at = pl.ds(pl.multiple_of(i * step, 16), step)
                e = dot(rf[i, 0:some * step, :], ct[j])
                total = None if phase == 0 else acc[j, at, :]
                for f in range(some):
                    one = e[f * step:(f + 1) * step]
                    sq = one * one
                    sq = sq[:, :block] + sq[:, block:]
                    total = sq if total is None else total + sq
                acc[j, at, :] = total

            if (phase, first, some) == groups[-1]:
                copy_s(j).start()

    for j in range(n_kern):
        copy_s(j).wait()
        out_ref[lax.rem(j + n_kern - my_k, n_kern)] = acc[j] + recv_s[j]


def bake_kernel(fields, coarse_ref, dh_ref, dl_ref, rates_ref, aer_hbm, lat_hbm, xs, aer, acid0, acid1, lat, sem):
    n_kern, ext, block = coarse_ref.shape
    rows, cols = aer_hbm.shape
    wide = dh_ref.shape[1]
    step = row_chunk(ext, 96)
    chunks = ext // step
    dill, arate, react, qstart = rates_ref[0], rates_ref[1], rates_ref[3], rates_ref[4]
    for j in range(n_kern):
        hi, lo = split(coarse_ref[j])
        xs[0:ext, j * block:(j + 1) * block] = hi
        xs[ext:2 * ext, j * block:(j + 1) * block] = lo
    tile = 384 if wide % 384 == 0 else 128
    for c in range(0, wide, tile):
        s = slice(c, c + tile)
        both = dot(xs[...], dh_ref[:, s])
        value = (both[:ext] + (both[ext:] + dot(xs[0:ext, :], dl_ref[:, s]))) * (1.0 / fields)
        aer[:, s] = value
        acid0[:, s] = 1.0 - jnp.exp((-4.0 * dill) * value)

    aer_out = pltpu.make_async_copy(aer.at[0:rows, 0:cols], aer_hbm, sem.at[0])
    aer_out.start()

    def laplace(ref, first, step):
        mid = ref[pl.ds(pl.multiple_of(first, 8), step), :]
        before = ref[pl.ds(pl.multiple_of(lax.rem(first + ext - 8, ext), 8), 8), :]
        after = ref[pl.ds(pl.multiple_of(lax.rem(first + step, ext), 8), 8), :]
        tall = jnp.concatenate([before, mid, after], 0)
        up = pltpu.roll(tall, 1, 0)[8:8 + step]
        down = pltpu.roll(tall, step + 15, 0)[8:8 + step]
        left = pltpu.roll(mid, 1, 1)
        right = pltpu.roll(mid, wide - 1, 1)
        return mid, down + up + right + left - 4.0 * mid

    @pl.loop(0, chunks)
    def _(i):
        mid, lap = laplace(acid0, i * step, step)
        value = mid + (arate * (0.5 + 0.5 * mid)) * lap - 4.0 * react * mid * qstart
        acid1[pl.ds(pl.multiple_of(i * step, 16), step), :] = value

    last = math.gcd(rows, 64)
    parts = rows // last

    def lat_out(i):
        at = pl.ds(pl.multiple_of(i * last, 16), last)
        return pltpu.make_async_copy(lat.at[at, :], lat_hbm.at[at, :], sem.at[1 + i])

    @pl.loop(0, parts)
    def _(i):
        at = pl.ds(pl.multiple_of(i * last, 16), last)
        mid, lap = laplace(acid1, i * last, last)
        first = acid0[at, :]
        quench = qstart - 4.0 * react * first * qstart
        value = mid + (arate * (0.5 + 0.5 * first)) * lap - 4.0 * react * mid * quench
        lat[at, :] = value[:, 0:cols]
        lat_out(i).start()

    aer_out.wait()

    @pl.loop(0, parts)
    def _(i):
        lat_out(i).wait()


def interpolation(cols, n):
    wide = cols + 2 * SIDE
    c = np.arange(wide)
    c = np.where(c < cols + SIDE, c, c - wide)
    ratio = n // COARSE
    t = c[None, :] - ratio * np.arange(COARSE)[:, None]
    zero = t % n == 0
    safe = np.where(zero, 1, t)
    d = np.sin(np.pi * (safe % (2 * ratio)) / ratio) / (COARSE * np.tan(np.pi * safe / n))
    d = np.where(zero, 1.0, np.where(t % ratio == 0, 0.0, d))
    hi = d.astype(jnp.bfloat16)
    lo = (d - hi.astype(np.float64)).astype(jnp.bfloat16)
    return hi, lo


def shards(n_kern, n_slab, layout, band_freqs, kernels, eigen_values, bake_rates):
    rows, cols = layout.shape
    fields, w = kernels.shape[1], kernels.shape[2]
    n = cols * n_kern
    ext = rows + 2 * HALO
    half = n_kern // 2
    block = COARSE // n_kern
    piece = 2 * w // n_slab
    step = row_chunk(ext, 192)
    chunks = ext // step
    vmem = pl.BlockSpec(memory_space=pltpu.VMEM)
    anyw = pl.BlockSpec(memory_space=pl.ANY)
    dma = pltpu.SemaphoreType.DMA
    coarse = pl.pallas_call(
        functools.partial(image_kernel, n_kern, n_slab),
        out_shape=jax.ShapeDtypeStruct((n_kern, ext, block), f32),
        in_specs=[anyw, vmem, anyw, pl.BlockSpec(memory_space=pltpu.SMEM)],
        out_specs=vmem,
        scratch_shapes=[
            pltpu.VMEM((rows, cols), jnp.int32),
            pltpu.VMEM((2, fields, w, w), f32),
            dma((2,)),
            pltpu.VMEM((half, fields, 2, w, w), f32),
            pltpu.VMEM((cols, 4 * w), bf16),
            pltpu.VMEM((2 * w, rows), bf16),
            pltpu.VMEM((2 * w, rows), bf16),
            pltpu.VMEM((ext, 2 * w), bf16),
            pltpu.VMEM((n_kern, 2 * w, 2 * block), bf16),
            pltpu.VMEM((n_slab, piece, w), f32),
            pltpu.VMEM((n_slab - 1, piece, w), f32),
            pltpu.VMEM((n_kern, piece, w), f32),
            pltpu.VMEM((n_slab, piece, w), f32),
            pltpu.VMEM((chunks, fields * step, 2 * w), bf16),
            pltpu.VMEM((n_kern, ext, block), f32),
            pltpu.VMEM((n_kern, ext, block), f32),
            dma((2, half)), dma((2, half)),
            dma((n_slab - 1,)), dma((n_slab - 1,)),
            dma((n_kern - 1,)), dma((n_kern - 1,)),
            dma((n_slab - 1,)), dma((n_slab - 1,)),
            dma((n_kern,)), dma((n_kern,)),
        ],
        compiler_params=pltpu.CompilerParams(
            collective_id=0, has_side_effects=True, vmem_limit_bytes=56 * 2**20),
        name="coarse_image",
    )(layout, band_freqs.reshape(1, w), kernels, eigen_values)
    dh, dl = interpolation(cols, n)
    wide = cols + 2 * SIDE
    return pl.pallas_call(
        functools.partial(bake_kernel, fields * n_kern),
        out_shape=[jax.ShapeDtypeStruct((rows, cols), f32)] * 2,
        in_specs=[vmem, vmem, vmem, pl.BlockSpec(memory_space=pltpu.SMEM)],
        out_specs=[anyw, anyw],
        scratch_shapes=[
            pltpu.VMEM((2 * ext, COARSE), bf16),
            pltpu.VMEM((ext, wide), f32),
            pltpu.VMEM((ext, wide), f32),
            pltpu.VMEM((ext, wide), f32),
            pltpu.VMEM((rows, cols), f32),
            dma((1 + rows // math.gcd(rows, 64),)),
        ],
        compiler_params=pltpu.CompilerParams(vmem_limit_bytes=34 * 2**20),
        name="interpolate_bake",
    )(coarse, jnp.asarray(dh), jnp.asarray(dl), bake_rates)


def solution(mesh):
    return jax.shard_map(
        functools.partial(shards, mesh.shape["kern"], mesh.shape["slab"]),
        mesh=mesh,
        in_specs=(P("slab", "kern"), P(), P(None, "kern", None, None), P("kern"), P()),
        out_specs=(P("slab", "kern"), P("slab", "kern")),
        check_vma=False,
    )
```
